32 devices in a mesh: wide: 8 (over z, y), seq: 4 (over x, core).
Axes of the slice: x: 2, y: 2, z: 4, core: 2. Of those that a mesh axis runs over, the one named last changes fastest.
Arguments:
- power: bfloat16 [160, 262144], P('seq', 'wide')
- bin_index: int32 [160], P('seq'), may hold values from 0 to 7, as said below
- session: int32 [2048], replicated, may hold values from 0 to 7, as said below
- readin_weight: bfloat16 [8, 128, 2048], P('wide'), may hold values from -0.5 to 0.5
- qkv_weight: bfloat16 [2048, 1536], replicated, may hold values from -0.125 to 0.125
Outputs:
- heads: bfloat16 [2048, 8, 1024], P(('wide', 'seq'))
The draws below stay inside these ranges and needn't reach their ends.
Inputs may be any that keep to these rules, and one draw needn't show every extreme that they name: `bin_index`: the samples j * 40 to (j + 1) * 40 - 1 name only bins j * 2 to (j + 1) * 2 - 1. In each aligned block of 64 patches (patches k * 64 to (k + 1) * 64 - 1) no session is named by more than 16 patches; one session, the same for every block, is named by exactly 16 patches of every block.
All inputs are finite; a program needn't handle non-finite values.
Results may differ from the reference program's by a relative error of at most 0.008.
Values may be sent and summed in bfloat16 or wider, within the bound.
A program may use at most 64 MiB of HBM per device.

```python
import math
import jax
import jax.numpy as jnp
from jax import lax

CH = 128
D = 2048
HD = 128
HEADS = 8
KVH = 2
SPB = 20
QP = 64
BIN_DEV = 2
QKV = 1536
PATCH_DEV = 256
SAMP_DEV = 40
BINS = 8
SAMPLES = 160
PATCHES = 2048
CHANNELS = 262144
SESSIONS = 8
CAP = 16
N_WIDE = 8


def draw_power(key, part):
    key_noise, key_rows, key_cols = jax.random.split(key, 3)
    moment = jnp.arange(SAMPLES, dtype=jnp.float32)
    rising = 1.0 + 2.0 * moment / max(SAMPLES - 1, 1)
    noise_part = jnp.exp(0.5 * jax.random.normal(key_noise, (SAMPLES, CHANNELS), jnp.float32))
    row_scale = jnp.exp(jax.random.uniform(key_rows, (SAMPLES,), jnp.float32, 0.0, math.log(10.0)))
    col_scale = jnp.exp(jax.random.uniform(key_cols, (CHANNELS,), jnp.float32, 0.0, math.log(10.0)))
    return (noise_part * (row_scale * rising)[:, None] * col_scale[None, :]).astype(jnp.bfloat16)


def draw_bin_index(key, part):
    moment = jnp.arange(SAMPLES, dtype=jnp.int32)
    shard_number = moment // SAMP_DEV
    inside = moment % SAMP_DEV
    jitter = jax.random.randint(key, (SAMPLES,), -4, 5)
    local_bin = jnp.clip((inside + jitter) // SPB, 0, BIN_DEV - 1)
    return (shard_number * BIN_DEV + local_bin).astype(jnp.int32)


def draw_session(key, part):
    key_hot, key_blocks = jax.random.split(key)
    block_total = PATCHES // QP
    hot_session = jax.random.randint(key_hot, (), 0, SESSIONS)
    others = jnp.arange((SESSIONS - 1) * CAP, dtype=jnp.int32) // CAP
    others = others + (others >= hot_session).astype(jnp.int32)

    def one_block(block_key):
        first_key, second_key = jax.random.split(block_key)
        picked = jax.random.permutation(first_key, others)[:QP - CAP]
        filled = jnp.concatenate([jnp.full((CAP,), hot_session, jnp.int32), picked])
        return jax.random.permutation(second_key, filled)
    blocks = jax.vmap(one_block)(jax.random.split(key_blocks, block_total))
    return blocks.reshape(PATCHES).astype(jnp.int32)


def level_of(own_key, dims, shards, least, high):
    level, own = 1.0, jax.random.fold_in(own_key, 6)
    for axis_at, blocks in shards:
        heights = jnp.exp(jax.random.uniform(jax.random.fold_in(own, axis_at), (blocks,), jnp.float32, least / len(shards), high / len(shards)))
        level = level * jnp.repeat(heights, dims[axis_at] // blocks).reshape([-1 if axis == axis_at else 1 for axis in range(len(dims))])
    return level


def noise(own_key, shape, deviation, most, pieces=(), kind=jnp.bfloat16):
    factor_of = level_of(own_key, shape, pieces, -0.22, 0.18) if pieces else 1.0
    drawn = jax.random.normal(own_key, shape, jnp.float32) * deviation * factor_of
    return jnp.minimum(jnp.maximum(drawn, -most), most).astype(kind)


def setup_inputs(seed: int = 0) -> dict:
    streams_of = jax.random.split(jax.random.key(seed), 6)
    power = draw_power(jax.random.fold_in(streams_of[5], 71), 0)
    bin_index = draw_bin_index(jax.random.fold_in(streams_of[5], 71), 0)
    session = draw_session(jax.random.fold_in(streams_of[5], 71), 0)
    readin_weight = noise(streams_of[3], (SESSIONS, CH, D), CH ** -0.5, 0.5, ((0, 8),))
    qkv_weight = noise(streams_of[4], (D, QKV), D ** -0.5, 0.125)
    return {"power": power, "bin_index": bin_index, "session": session, "readin_weight": readin_weight, "qkv_weight": qkv_weight}


def attention_heads(qkv_rows):
    row_count = qkv_rows.shape[0]
    length = qkv_rows.shape[1]
    group_size = HEADS // KVH
    values = qkv_rows.astype(jnp.float32)
    queries = values[:, :, :HEADS * HD].reshape(row_count, length, KVH, group_size, HD)
    key_rows = values[:, :, HEADS * HD:(HEADS + KVH) * HD].reshape(row_count, length, KVH, HD)
    value_rows = values[:, :, (HEADS + KVH) * HD:].reshape(row_count, length, KVH, HD)
    queries = queries / jnp.sqrt(lax.optimization_barrier(jnp.mean(queries * queries, axis=-1, keepdims=True)) + 1e-06)
    key_rows = key_rows / jnp.sqrt(lax.optimization_barrier(jnp.mean(key_rows * key_rows, axis=-1, keepdims=True)) + 1e-06)
    scores = jnp.einsum('pigrd,pjgd->pgrij', queries, key_rows) / HD ** 0.5
    exponent = jnp.exp(scores)
    weights = (exponent / lax.optimization_barrier(jnp.sum(exponent, axis=-1, keepdims=True))).astype(jnp.bfloat16)
    mixed = jnp.einsum('pgrij,pjgd->pigrd', weights.astype(jnp.float32), value_rows)
    return mixed.reshape(row_count, length, HEADS * HD).astype(jnp.bfloat16)

def reference(power, bin_index, session, readin_weight, qkv_weight):
    onehot = (bin_index[:, None] == jnp.arange(BINS, dtype=jnp.int32)[None, :]).astype(jnp.float32)
    block_width = PATCH_DEV * CH

    def one_column(column):
        power_block = lax.dynamic_slice_in_dim(power, column * block_width, block_width, 1).astype(jnp.float32)
        inv_rms = 1.0 / jnp.sqrt(lax.optimization_barrier(jnp.sum(power_block * power_block, axis=0)) / SAMPLES + 1e-06)
        active = jnp.maximum(power_block * inv_rms[None, :] - 0.8, 0.0)
        binned = (jnp.dot(onehot.T, active, precision=lax.Precision.HIGHEST) * (1.0 / SPB)).astype(jnp.bfloat16)
        patches = binned.reshape(BINS, PATCH_DEV, CH).transpose(1, 0, 2)
        owners = lax.dynamic_slice_in_dim(session, column * PATCH_DEV, PATCH_DEV).astype(jnp.int32)
        chosen = readin_weight[owners]
        tokens = jnp.einsum('pbc,pcd->pbd', patches.astype(jnp.float32), chosen.astype(jnp.float32)).astype(jnp.bfloat16)
        product = jnp.dot(tokens.reshape(PATCH_DEV * BINS, D), qkv_weight, preferred_element_type=jnp.float32)
        qkv_rows = product.astype(jnp.bfloat16).reshape(PATCH_DEV, BINS, QKV)
        return attention_heads(qkv_rows)
    columns = lax.map(one_column, jnp.arange(N_WIDE, dtype=jnp.int32))
    return columns.reshape(PATCHES, BINS, HEADS * HD)
```

```python
import jax
import jax.numpy as jnp
from jax import lax
from jax.sharding import PartitionSpec as P

CH = 128
HD = 128
HEADS = 8
KVH = 2
SPB = 20


def attention_rows(qkv, length):
    rows = qkv.shape[0]
    block = 16 * length
    group = HEADS // KVH
    values = qkv.astype(jnp.float32).reshape(rows, HEADS + 2 * KVH, HD)
    scored = values[:, : HEADS + KVH]
    normed = scored / jnp.sqrt(jnp.mean(scored * scored, axis=-1, keepdims=True) + 1e-06)
    normed = normed.astype(jnp.bfloat16).reshape(rows // block, block, HEADS + KVH, HD)
    queries = normed[:, :, :HEADS].reshape(rows // block, block, KVH, group, HD)
    scores = jnp.einsum(
        "nigrd,njgd->ngrij", queries, normed[:, :, HEADS:], preferred_element_type=jnp.float32
    ) / HD**0.5
    at = jnp.arange(block, dtype=jnp.int32) // length
    exponent = jnp.where(at[:, None] == at[None, :], jnp.exp(scores), 0.0)
    weights = (exponent / jnp.sum(exponent, axis=-1, keepdims=True)).astype(jnp.bfloat16)
    value_rows = qkv[:, (HEADS + KVH) * HD :].reshape(rows // block, block, KVH, HD)
    mixed = jnp.einsum(
        "ngrij,njgd->nigrd", weights, value_rows, preferred_element_type=jnp.float32
    )
    return mixed.astype(jnp.bfloat16).reshape(rows // length, length, HEADS * HD)


def body(power, bin_index, session, readin_weight, qkv_weight):
    wide_count = lax.axis_size("wide")
    seq_count = lax.axis_size("seq")
    wide_index = lax.axis_index("wide")
    seq_index = lax.axis_index("seq")
    sample_rows, channels = power.shape
    patch_count = channels // CH
    quarter = patch_count // seq_count
    bin_count = sample_rows // SPB
    columns = qkv_weight.shape[1] // seq_count

    signal = power.astype(jnp.float32)
    squares = lax.psum(jnp.sum(signal * signal, axis=0), "seq")
    inv_rms = 1.0 / jnp.sqrt(squares / (sample_rows * seq_count) + 1e-06)
    active = jnp.maximum(signal * inv_rms[None, :] - 0.8, 0.0)
    local_bins = bin_index - seq_index * bin_count
    onehot = (local_bins[:, None] == jnp.arange(bin_count, dtype=jnp.int32)[None, :]).astype(
        jnp.float32
    )
    binned = (jnp.dot(onehot.T, active, precision=lax.Precision.HIGHEST) * (1.0 / SPB)).astype(
        jnp.bfloat16
    )
    binned = binned.reshape(bin_count, seq_count, quarter, CH).transpose(1, 2, 0, 3)
    patches = lax.all_to_all(binned, "seq", split_axis=0, concat_axis=0, tiled=True)
    length = seq_count * bin_count
    rows = patches.transpose(1, 0, 2, 3).reshape(quarter, length, CH)
    owners = lax.dynamic_slice_in_dim(
        session, (wide_index * seq_count + seq_index) * quarter, quarter
    )
    marks = owners[:, None] == jnp.arange(wide_count, dtype=jnp.int32)[None, :]
    spread = jnp.where(marks[:, None, :, None], rows[:, :, None, :], jnp.bfloat16(0))
    spread = spread.reshape(quarter * length, wide_count * CH)

    def project(block):
        folded = jnp.dot(readin_weight[0], block, preferred_element_type=jnp.float32)
        folded = lax.all_gather(folded.astype(jnp.bfloat16), "wide", axis=0, tiled=True)
        return jnp.dot(spread, folded, preferred_element_type=jnp.float32).astype(jnp.bfloat16)

    if wide_count > 8:
        blocks = qkv_weight.reshape(qkv_weight.shape[0], seq_count, -1).transpose(1, 0, 2)
        qkv = lax.map(project, blocks).transpose(1, 0, 2).reshape(quarter * length, -1)
    else:
        qkv = project(qkv_weight)
    return attention_rows(qkv, length)


def solution(mesh):
    placed = (P("seq", "wide"), P("seq"), P(), P("wide", None, None), P())
    return jax.shard_map(
        body, mesh=mesh, in_specs=placed, out_specs=P(("wide", "seq"), None, None), check_vma=False
    )
```

```python
import jax
import jax.numpy as jnp
from jax import lax
from jax.experimental import pallas as pl
from jax.experimental.pallas import tpu as pltpu
from jax.sharding import PartitionSpec as P

CH = 128
HD = 128
HEADS = 8
KVH = 2
SPB = 20


def attention_rows(qkv, length):
    rows = qkv.shape[0]
    block = 16 * length
    group = HEADS // KVH
    values = qkv.astype(jnp.float32).reshape(rows, HEADS + 2 * KVH, HD)
    scored = values[:, : HEADS + KVH]
    normed = scored / jnp.sqrt(jnp.mean(scored * scored, axis=-1, keepdims=True) + 1e-06)
    normed = normed.astype(jnp.bfloat16).reshape(rows // block, block, HEADS + KVH, HD)
    queries = normed[:, :, :HEADS].reshape(rows // block, block, KVH, group, HD)
    scores = jnp.einsum(
        "nigrd,njgd->ngrij", queries, normed[:, :, HEADS:], preferred_element_type=jnp.float32
    ) / HD**0.5
    at = jnp.arange(block, dtype=jnp.int32) // length
    exponent = jnp.where(at[:, None] == at[None, :], jnp.exp(scores), 0.0)
    weights = (exponent / jnp.sum(exponent, axis=-1, keepdims=True)).astype(jnp.bfloat16)
    value_rows = qkv[:, (HEADS + KVH) * HD :].reshape(rows // block, block, KVH, HD)
    mixed = jnp.einsum(
        "ngrij,njgd->nigrd", weights, value_rows, preferred_element_type=jnp.float32
    )
    return mixed.astype(jnp.bfloat16).reshape(rows // length, length, HEADS * HD)


def body(power, bin_index, session, readin_weight, qkv_weight):
    wide_count = lax.axis_size("wide")
    seq_count = lax.axis_size("seq")
    wide_index = lax.axis_index("wide")
    seq_index = lax.axis_index("seq")
    sample_rows, channels = power.shape
    patch_count = channels // CH
    quarter = patch_count // seq_count
    bin_count = sample_rows // SPB
    columns = qkv_weight.shape[1] // seq_count

    signal = power.astype(jnp.float32)
    squares = lax.psum(jnp.sum(signal * signal, axis=0), "seq")
    inv_rms = 1.0 / jnp.sqrt(squares / (sample_rows * seq_count) + 1e-06)
    active = jnp.maximum(signal * inv_rms[None, :] - 0.8, 0.0)
    local_bins = bin_index - seq_index * bin_count
    onehot = (local_bins[:, None] == jnp.arange(bin_count, dtype=jnp.int32)[None, :]).astype(
        jnp.float32
    )
    binned = (jnp.dot(onehot.T, active, precision=lax.Precision.HIGHEST) * (1.0 / SPB)).astype(
        jnp.bfloat16
    )
    binned = binned.reshape(bin_count, seq_count, quarter, CH).transpose(1, 2, 0, 3)
    patches = lax.all_to_all(binned, "seq", split_axis=0, concat_axis=0, tiled=True)
    length = seq_count * bin_count
    rows = patches.transpose(1, 0, 2, 3).reshape(quarter, length, CH)
    owners = lax.dynamic_slice_in_dim(
        session, (wide_index * seq_count + seq_index) * quarter, quarter
    )
    marks = owners[:, None] == jnp.arange(wide_count, dtype=jnp.int32)[None, :]
    spread = jnp.where(marks[:, None, :, None], rows[:, :, None, :], jnp.bfloat16(0))
    spread = spread.reshape(quarter * length, wide_count * CH)

    def project(block):
        folded = jnp.dot(readin_weight[0], block, preferred_element_type=jnp.float32)
        folded = lax.all_gather(folded.astype(jnp.bfloat16), "wide", axis=0, tiled=True)
        return jnp.dot(spread, folded, preferred_element_type=jnp.float32).astype(jnp.bfloat16)

    if wide_count > 8:
        blocks = qkv_weight.reshape(qkv_weight.shape[0], seq_count, -1).transpose(1, 0, 2)
        qkv = lax.map(project, blocks).transpose(1, 0, 2).reshape(quarter * length, -1)
    else:
        qkv = project(qkv_weight)
    return attention_rows(qkv, length)


def kernel(
    power_hbm, bin_ref, session_ref, readin_hbm, weight_hbm, out_ref,
    power_v, readin_v, weight_v, folded, mask, spread, qkv,
    sq_own, sq_in, inv, bin_out, bin_in,
    load_sem, fold_send, fold_recv, seq_send, seq_recv,
):
    wide, seq = lax.axis_index("wide"), lax.axis_index("seq")
    seq_count, quarter, _ = sq_own.shape
    samples, channels = power_v.shape
    sessions = folded.shape[1]
    columns = folded.shape[3]
    bins = bin_out.shape[1] // quarter
    length = bins * seq_count
    z, y = lax.div(wide, 2), lax.rem(wide, 2)
    x, core = lax.div(seq, 2), lax.rem(seq, 2)
    flip_y, flip_x = 1 - 2 * y, 2 - 4 * x

    def paired(index, t):
        return (index, index + 1 - 2 * lax.rem(index, 2), lax.rem(index + 2, 4), 3 - index)[t]

    loads = [
        pltpu.make_async_copy(readin_hbm.at[0], readin_v, load_sem.at[4]),
        pltpu.make_async_copy(
            weight_hbm.at[:, pl.ds(pl.multiple_of(seq * columns, 128), columns)],
            weight_v,
            load_sem.at[5],
        ),
    ]
    for load in loads:
        load.start()
    part = channels // seq_count

    def power_load(q):
        at = pl.ds(pl.multiple_of(q * part, 128), part)
        return pltpu.make_async_copy(power_hbm.at[:, at], power_v.at[:, at], load_sem.at[q])

    for q in range(seq_count):
        power_load(q).start()

    barrier = pltpu.get_barrier_semaphore()

    def greet(device):
        pl.semaphore_signal(
            barrier, inc=1, device_id=device, device_id_type=pl.DeviceIdType.MESH
        )

    for d in range(1, 4):
        greet((wide, paired(seq, d)))
    greet((wide + flip_y, seq))

    @pl.when(z > 0)
    def _():
        greet((wide - 2, seq))

    @pl.when(z < 3)
    def _():
        greet((wide + 2, seq))

    for load in loads:
        load.wait()
    folded[seq, wide] = jnp.dot(
        readin_v[...], weight_v[...], preferred_element_type=jnp.float32
    ).astype(jnp.bfloat16)

    peers = 4 + jnp.where(z > 0, 1, 0) + jnp.where(z < 3, 1, 0)
    pl.semaphore_wait(barrier, peers)

    first = (wide + (1 - core) * flip_y, seq + core * flip_x)
    second = (wide + core * flip_y, seq + (1 - core) * flip_x)
    other_core = (wide, seq + 1 - 2 * core)
    lines = (
        (seq, y),
        (first[1], lax.rem(first[0], 2)),
        (second[1], lax.rem(second[0], 2)),
        (seq + flip_x, 1 - y),
    )

    def piece(line, t):
        return lines[line][0], paired(z, t) * 2 + lines[line][1]

    def fold_copy(at, sem, device):
        return pltpu.make_async_remote_copy(
            src_ref=folded.at[at[0], at[1]],
            dst_ref=folded.at[at[0], at[1]],
            send_sem=fold_send.at[sem],
            recv_sem=fold_recv.at[at[0], at[1]],
            device_id=device,
            device_id_type=pl.DeviceIdType.MESH,
        )

    def along_z(t, act):
        at = piece(0, t)
        here = paired(z, t)

        @pl.when(jnp.logical_and(here <= z, z < 3))
        def _():
            act(fold_copy(at, t, (wide + 2, seq)))

        @pl.when(jnp.logical_and(here >= z, z > 0))
        def _():
            act(fold_copy(at, 4 + t, (wide - 2, seq)))

    def onward(line, t, act):
        at = piece(line, t)
        if line == 0:
            act(fold_copy(at, 8 + t, first))
        if line < 2:
            act(fold_copy(at, 12 + 4 * line + t, second))
        act(fold_copy(at, 20 + 4 * line + t, other_core))

    def start(copy):
        copy.start()

    def wait_send(copy):
        copy.wait_send()

    def relay(line, t):
        if line or t:
            fold_copy(piece(line, t), 0, other_core).wait_recv()
        if line == 0:
            along_z(t, start)
        onward(line, t, start)

    relay(0, 0)

    def seq_copy(kind, source, target, d):
        return pltpu.make_async_remote_copy(
            src_ref=source,
            dst_ref=target,
            send_sem=seq_send.at[kind, d],
            recv_sem=seq_recv.at[kind, d],
            device_id=(wide, paired(seq, d)),
            device_id_type=pl.DeviceIdType.MESH,
        )

    def patch_rows(q, c):
        at = pl.multiple_of(q * part + c * 16 * CH, 16 * CH)
        return power_v[:, pl.ds(at, 16 * CH)].astype(jnp.float32)

    def square_copy(d):
        return seq_copy(0, sq_own.at[paired(seq, d)], sq_in.at[d], d)

    for d in (2, 3, 1, 0):
        q = paired(seq, d)
        power_load(q).wait()

        @pl.loop(0, quarter // 16)
        def _(c):
            signal = patch_rows(q, c)
            signal = signal * signal
            sums = [
                jnp.sum(signal[:, k * CH : (k + 1) * CH], axis=0, keepdims=True) for k in range(16)
            ]
            sq_own[q, pl.ds(pl.multiple_of(c * 16, 16), 16), :] = jnp.concatenate(sums, axis=0)

        if d:
            square_copy(d).start()

    rows = quarter * length
    device = wide * seq_count + seq
    session_row = session_ref[pl.ds(lax.div(device * quarter, 128), 1), :]
    named = (
        session_row == lax.broadcasted_iota(jnp.int32, (sessions, 128), 0)
    ).astype(jnp.bfloat16)
    lane = lax.broadcasted_iota(jnp.int32, (rows, 128), 1)
    row = lax.broadcasted_iota(jnp.int32, (rows, 128), 0)
    own = (
        lane == lax.rem(device * quarter, 128) + lax.div(row, length)
    ).astype(jnp.bfloat16)
    chosen = lax.dot_general(
        own, named, (((1,), (1,)), ((), ())), preferred_element_type=jnp.float32
    ).astype(jnp.bfloat16)
    widen = (
        lax.broadcasted_iota(jnp.int32, (sessions, sessions * CH), 0)
        == lax.div(lax.broadcasted_iota(jnp.int32, (sessions, sessions * CH), 1), CH)
    ).astype(jnp.bfloat16)
    mask[...] = jnp.dot(chosen, widen, preferred_element_type=jnp.float32).astype(jnp.bfloat16)

    diagonal = lax.broadcasted_iota(jnp.int32, (samples, samples), 0) == lax.broadcasted_iota(
        jnp.int32, (samples, samples), 1
    )
    local_bin = jnp.sum(
        jnp.where(diagonal, (bin_ref[...] - seq * bins).astype(jnp.float32), 0.0),
        axis=1,
        keepdims=True,
    )
    in_bin = [
        jnp.broadcast_to((local_bin == b).astype(jnp.float32), (samples, CH)) for b in range(bins)
    ]

    relay(0, 1)

    total = sq_own[seq]
    for d in range(1, 4):
        square_copy(d).wait_recv()
        total = total + sq_in[d]
    inv[0] = 1.0 / jnp.sqrt(total / (samples * seq_count) + 1e-06)

    def inv_copy(d):
        return seq_copy(1, inv.at[0], inv.at[d], d)

    for d in (2, 3, 1):
        inv_copy(d).start()

    def bin_quarter(d, target):
        q = paired(seq, d)

        @pl.loop(0, quarter // 16)
        def _(c):
            signal = patch_rows(q, c)
            at = pl.multiple_of(c * 16, 16)
            scale = inv[d, pl.ds(at, 16), :]
            found = [[] for _ in range(bins)]
            for k in range(16):
                active = jnp.maximum(
                    signal[:, k * CH : (k + 1) * CH] * scale[k : k + 1] - 0.8, 0.0
                )
                for b in range(bins):
                    found[b].append(jnp.sum(active * in_bin[b], axis=0, keepdims=True))
            for b in range(bins):
                target[d, pl.ds(pl.multiple_of(b * quarter + c * 16, 16), 16), :] = (
                    jnp.concatenate(found[b], axis=0) * (1.0 / SPB)
                ).astype(jnp.bfloat16)

    def bin_copy(d):
        return seq_copy(2, bin_out.at[d], bin_in.at[d], d)

    bin_quarter(0, bin_in)
    relay(0, 2)
    for d in (2, 3, 1):
        inv_copy(d).wait_recv()
        bin_quarter(d, bin_out)
        bin_copy(d).start()
        if d == 2:
            relay(0, 3)
            relay(1, 0)
        if d == 3:
            relay(1, 1)
    relay(1, 2)
    relay(1, 3)
    for t in range(4):
        relay(2, t)
    for t in range(4):
        relay(3, t)

    block = 16 * length
    r = lax.broadcasted_iota(jnp.int32, (block, block), 0)
    c = lax.broadcasted_iota(jnp.int32, (block, block), 1)
    turn = jnp.logical_and(
        lax.div(r, length) == lax.rem(c, 16), lax.rem(r, length) == lax.div(c, 16)
    ).astype(jnp.bfloat16)
    for d in range(1, 4):
        bin_copy(d).wait_recv()
    for n in range(quarter // 16):
        pieces = []
        for owner in range(seq_count):
            slot = owner + seq - 2 * (
                lax.rem(owner, 2) * lax.rem(seq, 2) + 2 * (owner // 2) * lax.div(seq, 2)
            )
            for b in range(bins):
                pieces.append(bin_in[slot, b * quarter + n * 16 : b * quarter + n * 16 + 16, :])
        turned = jnp.dot(
            turn, jnp.concatenate(pieces, axis=0), preferred_element_type=jnp.float32
        ).astype(jnp.bfloat16)
        at = slice(n * block, (n + 1) * block)
        spread[at, :] = mask[at, :] * jnp.concatenate([turned] * sessions, axis=1)

    for line in range(4):
        for t in range(4):
            at = piece(line, t)
            fold_copy((at[0] + 1 - 2 * core, at[1]), 0, other_core).wait_recv()

    for n in range(seq_count):
        weights = folded[n].reshape(sessions * CH, columns)
        qkv[:, n * columns : (n + 1) * columns] = jnp.dot(
            spread[...], weights, preferred_element_type=jnp.float32
        ).astype(jnp.bfloat16)

    group = HEADS // KVH
    same = lax.div(lax.broadcasted_iota(jnp.int32, (group * block, block), 0), length)
    same = lax.rem(same, 16) == lax.div(
        lax.broadcasted_iota(jnp.int32, (group * block, block), 1), length
    )

    @pl.loop(0, quarter // 16)
    def _(n):
        at = pl.ds(pl.multiple_of(n * block, block), block)

        def normed(h, scale):
            values = qkv[at, h * HD : (h + 1) * HD].astype(jnp.float32)
            mean = jnp.mean(values * values, axis=-1, keepdims=True)
            return (values * (lax.rsqrt(mean + 1e-06) * scale)).astype(jnp.bfloat16)

        for g in range(KVH):
            keys = normed(HEADS + g, 1.0)
            heads = range(g * group, (g + 1) * group)
            queries = jnp.concatenate([normed(h, HD**-0.5) for h in heads], axis=0)
            scores = lax.dot_general(
                queries, keys, (((1,), (1,)), ((), ())), preferred_element_type=jnp.float32
            )
            exponent = jnp.where(same, jnp.exp(scores), 0.0)
            weights = exponent * (1.0 / jnp.sum(exponent, axis=-1, keepdims=True))
            mixed = jnp.dot(
                weights.astype(jnp.bfloat16),
                qkv[at, (HEADS + KVH + g) * HD : (HEADS + KVH + g + 1) * HD],
                preferred_element_type=jnp.float32,
            )
            for i, h in enumerate(heads):
                own_rows = mixed[i * block : (i + 1) * block].reshape(16, length, HD)
                out_ref[pl.ds(n * 16, 16), :, h * HD : (h + 1) * HD] = own_rows.astype(
                    jnp.bfloat16
                )

    for d in range(1, 4):
        square_copy(d).wait_send()
        inv_copy(d).wait_send()
        bin_copy(d).wait_send()
    for line in range(4):
        for t in range(4):
            if line == 0:
                along_z(t, wait_send)
            onward(line, t, wait_send)


def fused(power, bin_index, session, readin_weight, qkv_weight):
    samples, channels = power.shape
    seq_count, sessions = lax.axis_size("seq"), lax.axis_size("wide")
    quarter = channels // CH // seq_count
    bins = samples // SPB
    columns = qkv_weight.shape[1] // seq_count
    rows = quarter * bins * seq_count
    width = readin_weight.shape[2]
    hbm = pl.BlockSpec(memory_space=pl.ANY)
    vmem = pl.BlockSpec(memory_space=pltpu.VMEM)
    bf16, f32 = jnp.bfloat16, jnp.float32
    dma = pltpu.SemaphoreType.DMA
    return pl.pallas_call(
        kernel,
        out_shape=jax.ShapeDtypeStruct((quarter, bins * seq_count, HEADS * HD), bf16),
        in_specs=[hbm, vmem, vmem, hbm, hbm],
        out_specs=vmem,
        scratch_shapes=[
            pltpu.VMEM((samples, channels), bf16),
            pltpu.VMEM((CH, width), bf16),
            pltpu.VMEM((width, columns), bf16),
            pltpu.VMEM((seq_count, sessions, CH, columns), bf16),
            pltpu.VMEM((rows, sessions * CH), bf16),
            pltpu.VMEM((rows, sessions * CH), bf16),
            pltpu.VMEM((rows, qkv_weight.shape[1]), bf16),
            pltpu.VMEM((seq_count, quarter, CH), f32),
            pltpu.VMEM((seq_count, quarter, CH), f32),
            pltpu.VMEM((seq_count, quarter, CH), f32),
            pltpu.VMEM((seq_count, bins * quarter, CH), bf16),
            pltpu.VMEM((seq_count, bins * quarter, CH), bf16),
            dma((6,)),
            dma((36,)),
            dma((seq_count, sessions)),
            dma((3, seq_count)),
            dma((3, seq_count)),
        ],
        compiler_params=pltpu.CompilerParams(
            collective_id=0, has_side_effects=True, vmem_limit_bytes=40 * 2**20
        ),
    )(power, bin_index.reshape(1, samples), session.reshape(-1, 128), readin_weight, qkv_weight)


def solution(mesh):
    fits = dict(mesh.shape) == {"wide": 8, "seq": 4}
    placed = (P("seq", "wide"), P("seq"), P(), P("wide", None, None), P())
    return jax.shard_map(
        fused if fits else body, mesh=mesh, in_specs=placed, out_specs=P(("wide", "seq"), None, None), check_vma=False
    )
```

```python
import jax
import jax.numpy as jnp
from jax import lax
from jax.experimental import pallas as pl
from jax.experimental.pallas import tpu as pltpu
from jax.sharding import PartitionSpec as P

CH = 128
HD = 128
HEADS = 8
KVH = 2
SPB = 20


def attention_rows(qkv, length):
    rows = qkv.shape[0]
    block = 16 * length
    group = HEADS // KVH
    values = qkv.astype(jnp.float32).reshape(rows, HEADS + 2 * KVH, HD)
    scored = values[:, : HEADS + KVH]
    normed = scored / jnp.sqrt(jnp.mean(scored * scored, axis=-1, keepdims=True) + 1e-06)
    normed = normed.astype(jnp.bfloat16).reshape(rows // block, block, HEADS + KVH, HD)
    queries = normed[:, :, :HEADS].reshape(rows // block, block, KVH, group, HD)
    scores = jnp.einsum(
        "nigrd,njgd->ngrij", queries, normed[:, :, HEADS:], preferred_element_type=jnp.float32
    ) / HD**0.5
    at = jnp.arange(block, dtype=jnp.int32) // length
    exponent = jnp.where(at[:, None] == at[None, :], jnp.exp(scores), 0.0)
    weights = (exponent / jnp.sum(exponent, axis=-1, keepdims=True)).astype(jnp.bfloat16)
    value_rows = qkv[:, (HEADS + KVH) * HD :].reshape(rows // block, block, KVH, HD)
    mixed = jnp.einsum(
        "ngrij,njgd->nigrd", weights, value_rows, preferred_element_type=jnp.float32
    )
    return mixed.astype(jnp.bfloat16).reshape(rows // length, length, HEADS * HD)


def body(power, bin_index, session, readin_weight, qkv_weight):
    wide_count = lax.axis_size("wide")
    seq_count = lax.axis_size("seq")
    wide_index = lax.axis_index("wide")
    seq_index = lax.axis_index("seq")
    sample_rows, channels = power.shape
    patch_count = channels // CH
    quarter = patch_count // seq_count
    bin_count = sample_rows // SPB
    columns = qkv_weight.shape[1] // seq_count

    signal = power.astype(jnp.float32)
    squares = lax.psum(jnp.sum(signal * signal, axis=0), "seq")
    inv_rms = 1.0 / jnp.sqrt(squares / (sample_rows * seq_count) + 1e-06)
    active = jnp.maximum(signal * inv_rms[None, :] - 0.8, 0.0)
    local_bins = bin_index - seq_index * bin_count
    onehot = (local_bins[:, None] == jnp.arange(bin_count, dtype=jnp.int32)[None, :]).astype(
        jnp.float32
    )
    binned = (jnp.dot(onehot.T, active, precision=lax.Precision.HIGHEST) * (1.0 / SPB)).astype(
        jnp.bfloat16
    )
    binned = binned.reshape(bin_count, seq_count, quarter, CH).transpose(1, 2, 0, 3)
    patches = lax.all_to_all(binned, "seq", split_axis=0, concat_axis=0, tiled=True)
    length = seq_count * bin_count
    rows = patches.transpose(1, 0, 2, 3).reshape(quarter, length, CH)
    owners = lax.dynamic_slice_in_dim(
        session, (wide_index * seq_count + seq_index) * quarter, quarter
    )
    marks = owners[:, None] == jnp.arange(wide_count, dtype=jnp.int32)[None, :]
    spread = jnp.where(marks[:, None, :, None], rows[:, :, None, :], jnp.bfloat16(0))
    spread = spread.reshape(quarter * length, wide_count * CH)

    def project(block):
        folded = jnp.dot(readin_weight[0], block, preferred_element_type=jnp.float32)
        folded = lax.all_gather(folded.astype(jnp.bfloat16), "wide", axis=0, tiled=True)
        return jnp.dot(spread, folded, preferred_element_type=jnp.float32).astype(jnp.bfloat16)

    if wide_count > 8:
        blocks = qkv_weight.reshape(qkv_weight.shape[0], seq_count, -1).transpose(1, 0, 2)
        qkv = lax.map(project, blocks).transpose(1, 0, 2).reshape(quarter * length, -1)
    else:
        qkv = project(qkv_weight)
    return attention_rows(qkv, length)


def kernel(
    power_hbm, bin_hbm, session_hbm, readin_hbm, weight_hbm, out_ref,
    bin_ref, session_ref,
    power_v, readin_v, weight_v, folded, mask, spread, qkv,
    sq_own, sq_in, inv, bin_out, bin_in,
    load_sem, fold_send, fold_recv, seq_send, seq_recv,
):
    wide, seq = lax.axis_index("wide"), lax.axis_index("seq")
    seq_count, quarter, _ = sq_own.shape
    samples, channels = power_v.shape
    sessions = folded.shape[1]
    columns = folded.shape[3]
    bins = bin_out.shape[1] // quarter
    length = bins * seq_count
    z, y = lax.div(wide, 2), lax.rem(wide, 2)
    x, core = lax.div(seq, 2), lax.rem(seq, 2)
    flip_y, flip_x = 1 - 2 * y, 2 - 4 * x

    def paired(index, t):
        return (index, index + 1 - 2 * lax.rem(index, 2), lax.rem(index + 2, 4), 3 - index)[t]

    loads = [
        pltpu.make_async_copy(readin_hbm.at[0], readin_v, load_sem.at[4]),
        pltpu.make_async_copy(
            weight_hbm.at[:, pl.ds(pl.multiple_of(seq * columns, 128), columns)],
            weight_v,
            load_sem.at[5],
        ),
    ]
    for load in loads:
        load.start()
    part = channels // seq_count

    def power_load(q):
        at = pl.ds(pl.multiple_of(q * part, 128), part)
        return pltpu.make_async_copy(power_hbm.at[:, at], power_v.at[:, at], load_sem.at[q])

    for q in range(seq_count):
        power_load(q).start()

    indices = [
        pltpu.make_async_copy(bin_hbm, bin_ref, load_sem.at[6]),
        pltpu.make_async_copy(session_hbm, session_ref, load_sem.at[7]),
    ]
    for load in indices:
        load.start()

    barrier = pltpu.get_barrier_semaphore()

    def greet(device):
        pl.semaphore_signal(
            barrier, inc=1, device_id=device, device_id_type=pl.DeviceIdType.MESH
        )

    for d in range(1, 4):
        greet((wide, paired(seq, d)))
    greet((wide + flip_y, seq))

    @pl.when(z > 0)
    def _():
        greet((wide - 2, seq))

    @pl.when(z < 3)
    def _():
        greet((wide + 2, seq))

    for load in loads:
        load.wait()
    folded[seq, wide] = jnp.dot(
        readin_v[...], weight_v[...], preferred_element_type=jnp.float32
    ).astype(jnp.bfloat16)

    peers = 4 + jnp.where(z > 0, 1, 0) + jnp.where(z < 3, 1, 0)
    pl.semaphore_wait(barrier, peers)

    first = (wide + (1 - core) * flip_y, seq + core * flip_x)
    second = (wide + core * flip_y, seq + (1 - core) * flip_x)
    other_core = (wide, seq + 1 - 2 * core)
    lines = (
        (seq, y),
        (first[1], lax.rem(first[0], 2)),
        (second[1], lax.rem(second[0], 2)),
        (seq + flip_x, 1 - y),
    )

    nearest = (z, 1 + lax.rem(z, 2), lax.rem(2 + 3 * z, 5), 3 - 3 * lax.div(z, 2))

    def piece(line, t):
        return lines[line][0], nearest[t] * 2 + lines[line][1]

    def fold_copy(at, sem, device):
        return pltpu.make_async_remote_copy(
            src_ref=folded.at[at[0], at[1]],
            dst_ref=folded.at[at[0], at[1]],
            send_sem=fold_send.at[sem],
            recv_sem=fold_recv.at[at[0], at[1]],
            device_id=device,
            device_id_type=pl.DeviceIdType.MESH,
        )

    def along_z(t, act):
        at = piece(0, t)
        here = nearest[t]

        @pl.when(jnp.logical_and(here <= z, z < 3))
        def _():
            act(fold_copy(at, t, (wide + 2, seq)))

        @pl.when(jnp.logical_and(here >= z, z > 0))
        def _():
            act(fold_copy(at, 4 + t, (wide - 2, seq)))

    def onward(line, t, act):
        at = piece(line, t)
        if line == 0:
            act(fold_copy(at, 8 + t, first))
        if line < 2:
            act(fold_copy(at, 12 + 4 * line + t, second))
        act(fold_copy(at, 20 + 4 * line + t, other_core))

    def start(copy):
        copy.start()

    def wait_send(copy):
        copy.wait_send()

    def relay(line, t):
        if line or t:
            fold_copy(piece(line, t), 0, other_core).wait_recv()
        if line == 0:
            along_z(t, start)
        onward(line, t, start)

    relay(0, 0)

    def seq_copy(kind, source, target, d):
        return pltpu.make_async_remote_copy(
            src_ref=source,
            dst_ref=target,
            send_sem=seq_send.at[kind, d],
            recv_sem=seq_recv.at[kind, d],
            device_id=(wide, paired(seq, d)),
            device_id_type=pl.DeviceIdType.MESH,
        )

    def patch_rows(q, c):
        at = pl.multiple_of(q * part + c * 16 * CH, 16 * CH)
        return power_v[:, pl.ds(at, 16 * CH)].astype(jnp.float32)

    def square_copy(d):
        return seq_copy(0, sq_own.at[paired(seq, d)], sq_in.at[d], d)

    for d in (2, 3, 1, 0):
        q = paired(seq, d)
        power_load(q).wait()

        @pl.loop(0, quarter // 16)
        def _(c):
            signal = patch_rows(q, c)
            signal = signal * signal
            sums = [
                jnp.sum(signal[:, k * CH : (k + 1) * CH], axis=0, keepdims=True) for k in range(16)
            ]
            sq_own[q, pl.ds(pl.multiple_of(c * 16, 16), 16), :] = jnp.concatenate(sums, axis=0)

        if d:
            square_copy(d).start()

    relay(0, 1)
    for load in indices:
        load.wait()

    rows = quarter * length
    device = wide * seq_count + seq
    session_row = session_ref[pl.ds(lax.div(device * quarter, 128), 1), :]
    named = (
        session_row == lax.broadcasted_iota(jnp.int32, (sessions, 128), 0)
    ).astype(jnp.bfloat16)
    lane = lax.broadcasted_iota(jnp.int32, (rows, 128), 1)
    row = lax.broadcasted_iota(jnp.int32, (rows, 128), 0)
    own = (
        lane == lax.rem(device * quarter, 128) + lax.div(row, length)
    ).astype(jnp.bfloat16)
    chosen = lax.dot_general(
        own, named, (((1,), (1,)), ((), ())), preferred_element_type=jnp.float32
    ).astype(jnp.bfloat16)
    widen = (
        lax.broadcasted_iota(jnp.int32, (sessions, sessions * CH), 0)
        == lax.div(lax.broadcasted_iota(jnp.int32, (sessions, sessions * CH), 1), CH)
    ).astype(jnp.bfloat16)
    mask[...] = jnp.dot(chosen, widen, preferred_element_type=jnp.float32).astype(jnp.bfloat16)

    diagonal = lax.broadcasted_iota(jnp.int32, (samples, samples), 0) == lax.broadcasted_iota(
        jnp.int32, (samples, samples), 1
    )
    local_bin = jnp.sum(
        jnp.where(diagonal, (bin_ref[...] - seq * bins).astype(jnp.float32), 0.0),
        axis=1,
        keepdims=True,
    )
    in_bin = [
        jnp.broadcast_to((local_bin == b).astype(jnp.float32), (samples, CH)) for b in range(bins)
    ]

    relay(0, 2)

    total = sq_own[seq]
    for d in range(1, 4):
        square_copy(d).wait_recv()
        total = total + sq_in[d]
    inv[0] = 1.0 / jnp.sqrt(total / (samples * seq_count) + 1e-06)

    def inv_copy(d):
        return seq_copy(1, inv.at[0], inv.at[d], d)

    for d in (2, 3, 1):
        inv_copy(d).start()

    def bin_quarter(d, target):
        q = paired(seq, d)

        @pl.loop(0, quarter // 16)
        def _(c):
            signal = patch_rows(q, c)
            at = pl.multiple_of(c * 16, 16)
            scale = inv[d, pl.ds(at, 16), :]
            found = [[] for _ in range(bins)]
            for k in range(16):
                active = jnp.maximum(
                    signal[:, k * CH : (k + 1) * CH] * scale[k : k + 1] - 0.8, 0.0
                )
                for b in range(bins):
                    found[b].append(jnp.sum(active * in_bin[b], axis=0, keepdims=True))
            for b in range(bins):
                target[d, pl.ds(pl.multiple_of(b * quarter + c * 16, 16), 16), :] = (
                    jnp.concatenate(found[b], axis=0) * (1.0 / SPB)
                ).astype(jnp.bfloat16)

    def bin_copy(d):
        return seq_copy(2, bin_out.at[d], bin_in.at[d], d)

    relay(0, 3)
    relay(1, 0)
    bin_quarter(0, bin_in)
    relay(1, 1)
    for d in (2, 3, 1):
        inv_copy(d).wait_recv()
        bin_quarter(d, bin_out)
        bin_copy(d).start()
        if d == 2:
            relay(1, 2)
        if d == 3:
            relay(1, 3)
    for t in range(4):
        relay(2, t)
    for t in range(4):
        relay(3, t)

    block = 16 * length
    r = lax.broadcasted_iota(jnp.int32, (block, block), 0)
    c = lax.broadcasted_iota(jnp.int32, (block, block), 1)
    turn = jnp.logical_and(
        lax.div(r, length) == lax.rem(c, 16), lax.rem(r, length) == lax.div(c, 16)
    ).astype(jnp.bfloat16)
    for d in range(1, 4):
        bin_copy(d).wait_recv()
    for n in range(quarter // 16):
        pieces = []
        for owner in range(seq_count):
            slot = owner + seq - 2 * (
                lax.rem(owner, 2) * lax.rem(seq, 2) + 2 * (owner // 2) * lax.div(seq, 2)
            )
            for b in range(bins):
                pieces.append(bin_in[slot, b * quarter + n * 16 : b * quarter + n * 16 + 16, :])
        turned = jnp.dot(
            turn, jnp.concatenate(pieces, axis=0), preferred_element_type=jnp.float32
        ).astype(jnp.bfloat16)
        at = slice(n * block, (n + 1) * block)
        spread[at, :] = mask[at, :] * jnp.concatenate([turned] * sessions, axis=1)

    for line in range(4):
        for t in range(4):
            at = piece(line, t)
            fold_copy((at[0] + 1 - 2 * core, at[1]), 0, other_core).wait_recv()

    for n in range(seq_count):
        weights = folded[n].reshape(sessions * CH, columns)
        qkv[:, n * columns : (n + 1) * columns] = jnp.dot(
            spread[...], weights, preferred_element_type=jnp.float32
        ).astype(jnp.bfloat16)

    group = HEADS // KVH
    same = lax.div(lax.broadcasted_iota(jnp.int32, (group * block, block), 0), length)
    same = lax.rem(same, 16) == lax.div(
        lax.broadcasted_iota(jnp.int32, (group * block, block), 1), length
    )

    @pl.loop(0, quarter // 16)
    def _(n):
        at = pl.ds(pl.multiple_of(n * block, block), block)

        def normed(h, scale):
            values = qkv[at, h * HD : (h + 1) * HD].astype(jnp.float32)
            mean = jnp.mean(values * values, axis=-1, keepdims=True)
            return (values * (lax.rsqrt(mean + 1e-06) * scale)).astype(jnp.bfloat16)

        for g in range(KVH):
            keys = normed(HEADS + g, 1.0)
            heads = range(g * group, (g + 1) * group)
            queries = jnp.concatenate([normed(h, HD**-0.5) for h in heads], axis=0)
            scores = lax.dot_general(
                queries, keys, (((1,), (1,)), ((), ())), preferred_element_type=jnp.float32
            )
            exponent = jnp.where(same, jnp.exp(scores), 0.0)
            weights = exponent * (1.0 / jnp.sum(exponent, axis=-1, keepdims=True))
            mixed = jnp.dot(
                weights.astype(jnp.bfloat16),
                qkv[at, (HEADS + KVH + g) * HD : (HEADS + KVH + g + 1) * HD],
                preferred_element_type=jnp.float32,
            )
            for i, h in enumerate(heads):
                own_rows = mixed[i * block : (i + 1) * block].reshape(16, length, HD)
                out_ref[pl.ds(n * 16, 16), :, h * HD : (h + 1) * HD] = own_rows.astype(
                    jnp.bfloat16
                )

    for d in range(1, 4):
        square_copy(d).wait_send()
        inv_copy(d).wait_send()
        bin_copy(d).wait_send()
    for line in range(4):
        for t in range(4):
            if line == 0:
                along_z(t, wait_send)
            onward(line, t, wait_send)


def fused(power, bin_index, session, readin_weight, qkv_weight):
    samples, channels = power.shape
    seq_count, sessions = lax.axis_size("seq"), lax.axis_size("wide")
    quarter = channels // CH // seq_count
    bins = samples // SPB
    columns = qkv_weight.shape[1] // seq_count
    rows = quarter * bins * seq_count
    width = readin_weight.shape[2]
    hbm = pl.BlockSpec(memory_space=pltpu.HBM)
    vmem = pl.BlockSpec(memory_space=pltpu.VMEM)
    bf16, f32 = jnp.bfloat16, jnp.float32
    dma = pltpu.SemaphoreType.DMA
    return pl.pallas_call(
        kernel,
        out_shape=jax.ShapeDtypeStruct((quarter, bins * seq_count, HEADS * HD), bf16),
        in_specs=[hbm] * 5,
        out_specs=vmem,
        scratch_shapes=[
            pltpu.VMEM((1, samples), jnp.int32),
            pltpu.VMEM((session.shape[0] // 128, 128), jnp.int32),
            pltpu.VMEM((samples, channels), bf16),
            pltpu.VMEM((CH, width), bf16),
            pltpu.VMEM((width, columns), bf16),
            pltpu.VMEM((seq_count, sessions, CH, columns), bf16),
            pltpu.VMEM((rows, sessions * CH), bf16),
            pltpu.VMEM((rows, sessions * CH), bf16),
            pltpu.VMEM((rows, qkv_weight.shape[1]), bf16),
            pltpu.VMEM((seq_count, quarter, CH), f32),
            pltpu.VMEM((seq_count, quarter, CH), f32),
            pltpu.VMEM((seq_count, quarter, CH), f32),
            pltpu.VMEM((seq_count, bins * quarter, CH), bf16),
            pltpu.VMEM((seq_count, bins * quarter, CH), bf16),
            dma((8,)),
            dma((36,)),
            dma((seq_count, sessions)),
            dma((3, seq_count)),
            dma((3, seq_count)),
        ],
        compiler_params=pltpu.CompilerParams(
            collective_id=0, has_side_effects=True, vmem_limit_bytes=56 * 2**20
        ),
    )(power, bin_index.reshape(1, samples), session.reshape(-1, 128), readin_weight, qkv_weight)


def solution(mesh):
    fits = dict(mesh.shape) == {"wide": 8, "seq": 4}
    placed = (P("seq", "wide"), P("seq"), P(), P("wide", None, None), P())
    return jax.shard_map(
        fused if fits else body, mesh=mesh, in_specs=placed, out_specs=P(("wide", "seq"), None, None), check_vma=False
    )
```

```python
import jax
import jax.numpy as jnp
from jax import lax
from jax.experimental import pallas as pl
from jax.experimental.pallas import tpu as pltpu
from jax.sharding import PartitionSpec as P

CH = 128
HD = 128
HEADS = 8
KVH = 2
SPB = 20


def attention_rows(qkv, length):
    rows = qkv.shape[0]
    block = 16 * length
    group = HEADS // KVH
    values = qkv.astype(jnp.float32).reshape(rows, HEADS + 2 * KVH, HD)
    scored = values[:, : HEADS + KVH]
    normed = scored / jnp.sqrt(jnp.mean(scored * scored, axis=-1, keepdims=True) + 1e-06)
    normed = normed.astype(jnp.bfloat16).reshape(rows // block, block, HEADS + KVH, HD)
    queries = normed[:, :, :HEADS].reshape(rows // block, block, KVH, group, HD)
    scores = jnp.einsum(
        "nigrd,njgd->ngrij", queries, normed[:, :, HEADS:], preferred_element_type=jnp.float32
    ) / HD**0.5
    at = jnp.arange(block, dtype=jnp.int32) // length
    exponent = jnp.where(at[:, None] == at[None, :], jnp.exp(scores), 0.0)
    weights = (exponent / jnp.sum(exponent, axis=-1, keepdims=True)).astype(jnp.bfloat16)
    value_rows = qkv[:, (HEADS + KVH) * HD :].reshape(rows // block, block, KVH, HD)
    mixed = jnp.einsum(
        "ngrij,njgd->nigrd", weights, value_rows, preferred_element_type=jnp.float32
    )
    return mixed.astype(jnp.bfloat16).reshape(rows // length, length, HEADS * HD)


def body(power, bin_index, session, readin_weight, qkv_weight):
    wide_count = lax.axis_size("wide")
    seq_count = lax.axis_size("seq")
    wide_index = lax.axis_index("wide")
    seq_index = lax.axis_index("seq")
    sample_rows, channels = power.shape
    patch_count = channels // CH
    quarter = patch_count // seq_count
    bin_count = sample_rows // SPB
    columns = qkv_weight.shape[1] // seq_count

    signal = power.astype(jnp.float32)
    squares = lax.psum(jnp.sum(signal * signal, axis=0), "seq")
    inv_rms = 1.0 / jnp.sqrt(squares / (sample_rows * seq_count) + 1e-06)
    active = jnp.maximum(signal * inv_rms[None, :] - 0.8, 0.0)
    local_bins = bin_index - seq_index * bin_count
    onehot = (local_bins[:, None] == jnp.arange(bin_count, dtype=jnp.int32)[None, :]).astype(
        jnp.float32
    )
    binned = (jnp.dot(onehot.T, active, precision=lax.Precision.HIGHEST) * (1.0 / SPB)).astype(
        jnp.bfloat16
    )
    binned = binned.reshape(bin_count, seq_count, quarter, CH).transpose(1, 2, 0, 3)
    patches = lax.all_to_all(binned, "seq", split_axis=0, concat_axis=0, tiled=True)
    length = seq_count * bin_count
    rows = patches.transpose(1, 0, 2, 3).reshape(quarter, length, CH)
    owners = lax.dynamic_slice_in_dim(
        session, (wide_index * seq_count + seq_index) * quarter, quarter
    )
    marks = owners[:, None] == jnp.arange(wide_count, dtype=jnp.int32)[None, :]
    spread = jnp.where(marks[:, None, :, None], rows[:, :, None, :], jnp.bfloat16(0))
    spread = spread.reshape(quarter * length, wide_count * CH)

    def project(block):
        folded = jnp.dot(readin_weight[0], block, preferred_element_type=jnp.float32)
        folded = lax.all_gather(folded.astype(jnp.bfloat16), "wide", axis=0, tiled=True)
        return jnp.dot(spread, folded, preferred_element_type=jnp.float32).astype(jnp.bfloat16)

    if wide_count > 8:
        blocks = qkv_weight.reshape(qkv_weight.shape[0], seq_count, -1).transpose(1, 0, 2)
        qkv = lax.map(project, blocks).transpose(1, 0, 2).reshape(quarter * length, -1)
    else:
        qkv = project(qkv_weight)
    return attention_rows(qkv, length)


def kernel(
    power_hbm, bin_hbm, session_hbm, readin_hbm, weight_hbm, qkv_ref,
    bin_ref, session_ref,
    power_v, readin_v, weight_v, folded, mask, spread,
    sq_own, sq_in, inv, bin_out, bin_in,
    load_sem, fold_send, fold_recv, seq_send, seq_recv,
):
    wide, seq = lax.axis_index("wide"), lax.axis_index("seq")
    seq_count, quarter, _ = sq_own.shape
    samples, channels = power_v.shape
    sessions = folded.shape[1]
    columns = folded.shape[3]
    bins = bin_out.shape[1] // quarter
    length = bins * seq_count
    z, y = lax.div(wide, 2), lax.rem(wide, 2)
    x, core = lax.div(seq, 2), lax.rem(seq, 2)
    flip_y, flip_x = 1 - 2 * y, 2 - 4 * x

    def paired(index, t):
        return (index, index + 1 - 2 * lax.rem(index, 2), lax.rem(index + 2, 4), 3 - index)[t]

    loads = [
        pltpu.make_async_copy(readin_hbm.at[0], readin_v, load_sem.at[4]),
        pltpu.make_async_copy(
            weight_hbm.at[:, pl.ds(pl.multiple_of(seq * columns, 128), columns)],
            weight_v,
            load_sem.at[5],
        ),
    ]
    for load in loads:
        load.start()
    part = channels // seq_count

    def power_load(q):
        at = pl.ds(pl.multiple_of(q * part, 128), part)
        return pltpu.make_async_copy(power_hbm.at[:, at], power_v.at[:, at], load_sem.at[q])

    for q in range(seq_count):
        power_load(q).start()

    indices = [
        pltpu.make_async_copy(bin_hbm, bin_ref, load_sem.at[6]),
        pltpu.make_async_copy(session_hbm, session_ref, load_sem.at[7]),
    ]
    for load in indices:
        load.start()

    barrier = pltpu.get_barrier_semaphore()

    def greet(device):
        pl.semaphore_signal(
            barrier, inc=1, device_id=device, device_id_type=pl.DeviceIdType.MESH
        )

    for d in range(1, 4):
        greet((wide, paired(seq, d)))
    greet((wide + flip_y, seq))

    @pl.when(z > 0)
    def _():
        greet((wide - 2, seq))

    @pl.when(z < 3)
    def _():
        greet((wide + 2, seq))

    for load in loads:
        load.wait()
    folded[seq, wide] = jnp.dot(
        readin_v[...], weight_v[...], preferred_element_type=jnp.float32
    ).astype(jnp.bfloat16)

    peers = 4 + jnp.where(z > 0, 1, 0) + jnp.where(z < 3, 1, 0)
    pl.semaphore_wait(barrier, peers)

    first = (wide + (1 - core) * flip_y, seq + core * flip_x)
    second = (wide + core * flip_y, seq + (1 - core) * flip_x)
    other_core = (wide, seq + 1 - 2 * core)
    lines = (
        (seq, y),
        (first[1], lax.rem(first[0], 2)),
        (second[1], lax.rem(second[0], 2)),
        (seq + flip_x, 1 - y),
    )

    nearest = (z, 1 + lax.rem(z, 2), lax.rem(2 + 3 * z, 5), 3 - 3 * lax.div(z, 2))

    def piece(line, t):
        return lines[line][0], nearest[t] * 2 + lines[line][1]

    def fold_copy(at, sem, device):
        return pltpu.make_async_remote_copy(
            src_ref=folded.at[at[0], at[1]],
            dst_ref=folded.at[at[0], at[1]],
            send_sem=fold_send.at[sem],
            recv_sem=fold_recv.at[at[0], at[1]],
            device_id=device,
            device_id_type=pl.DeviceIdType.MESH,
        )

    def along_z(t, act):
        at = piece(0, t)
        here = nearest[t]

        @pl.when(jnp.logical_and(here <= z, z < 3))
        def _():
            act(fold_copy(at, t, (wide + 2, seq)))

        @pl.when(jnp.logical_and(here >= z, z > 0))
        def _():
            act(fold_copy(at, 4 + t, (wide - 2, seq)))

    def onward(line, t, act):
        at = piece(line, t)
        if line == 0:
            act(fold_copy(at, 8 + t, first))
        if line < 2:
            act(fold_copy(at, 12 + 4 * line + t, second))
        act(fold_copy(at, 20 + 4 * line + t, other_core))

    def start(copy):
        copy.start()

    def wait_send(copy):
        copy.wait_send()

    def relay(line, t):
        if line or t:
            fold_copy(piece(line, t), 0, other_core).wait_recv()
        if line == 0:
            along_z(t, start)
        onward(line, t, start)

    relay(0, 0)

    def seq_copy(kind, source, target, d):
        return pltpu.make_async_remote_copy(
            src_ref=source,
            dst_ref=target,
            send_sem=seq_send.at[kind, d],
            recv_sem=seq_recv.at[kind, d],
            device_id=(wide, paired(seq, d)),
            device_id_type=pl.DeviceIdType.MESH,
        )

    def patch_rows(q, c):
        at = pl.multiple_of(q * part + c * 16 * CH, 16 * CH)
        return power_v[:, pl.ds(at, 16 * CH)].astype(jnp.float32)

    def square_copy(d):
        return seq_copy(0, sq_own.at[paired(seq, d)], sq_in.at[d], d)

    for d in (2, 3, 1, 0):
        q = paired(seq, d)
        power_load(q).wait()

        @pl.loop(0, quarter // 16)
        def _(c):
            signal = patch_rows(q, c)
            signal = signal * signal
            sums = [
                jnp.sum(signal[:, k * CH : (k + 1) * CH], axis=0, keepdims=True) for k in range(16)
            ]
            sq_own[q, pl.ds(pl.multiple_of(c * 16, 16), 16), :] = jnp.concatenate(sums, axis=0)

        if d:
            square_copy(d).start()

    relay(0, 1)
    for load in indices:
        load.wait()

    rows = quarter * length
    device = wide * seq_count + seq
    session_row = session_ref[pl.ds(lax.div(device * quarter, 128), 1), :]
    named = (
        session_row == lax.broadcasted_iota(jnp.int32, (sessions, 128), 0)
    ).astype(jnp.bfloat16)
    lane = lax.broadcasted_iota(jnp.int32, (rows, 128), 1)
    row = lax.broadcasted_iota(jnp.int32, (rows, 128), 0)
    own = (
        lane == lax.rem(device * quarter, 128) + lax.div(row, length)
    ).astype(jnp.bfloat16)
    chosen = lax.dot_general(
        own, named, (((1,), (1,)), ((), ())), preferred_element_type=jnp.float32
    ).astype(jnp.bfloat16)
    widen = (
        lax.broadcasted_iota(jnp.int32, (sessions, sessions * CH), 0)
        == lax.div(lax.broadcasted_iota(jnp.int32, (sessions, sessions * CH), 1), CH)
    ).astype(jnp.bfloat16)
    mask[...] = jnp.dot(chosen, widen, preferred_element_type=jnp.float32).astype(jnp.bfloat16)

    diagonal = lax.broadcasted_iota(jnp.int32, (samples, samples), 0) == lax.broadcasted_iota(
        jnp.int32, (samples, samples), 1
    )
    local_bin = jnp.sum(
        jnp.where(diagonal, (bin_ref[...] - seq * bins).astype(jnp.float32), 0.0),
        axis=1,
        keepdims=True,
    )
    in_bin = [
        jnp.broadcast_to((local_bin == b).astype(jnp.float32), (samples, CH)) for b in range(bins)
    ]

    relay(0, 2)

    total = sq_own[seq]
    for d in range(1, 4):
        square_copy(d).wait_recv()
        total = total + sq_in[d]
    inv[0] = 1.0 / jnp.sqrt(total / (samples * seq_count) + 1e-06)

    def inv_copy(d):
        return seq_copy(1, inv.at[0], inv.at[d], d)

    for d in (2, 3, 1):
        inv_copy(d).start()

    def bin_quarter(d, target):
        q = paired(seq, d)

        @pl.loop(0, quarter // 16)
        def _(c):
            signal = patch_rows(q, c)
            at = pl.multiple_of(c * 16, 16)
            scale = inv[d, pl.ds(at, 16), :]
            found = [[] for _ in range(bins)]
            for k in range(16):
                active = jnp.maximum(
                    signal[:, k * CH : (k + 1) * CH] * scale[k : k + 1] - 0.8, 0.0
                )
                for b in range(bins):
                    found[b].append(jnp.sum(active * in_bin[b], axis=0, keepdims=True))
            for b in range(bins):
                target[d, pl.ds(pl.multiple_of(b * quarter + c * 16, 16), 16), :] = (
                    jnp.concatenate(found[b], axis=0) * (1.0 / SPB)
                ).astype(jnp.bfloat16)

    def bin_copy(d):
        return seq_copy(2, bin_out.at[d], bin_in.at[d], d)

    relay(0, 3)
    relay(1, 0)
    bin_quarter(0, bin_in)
    relay(1, 1)
    for d in (2, 3, 1):
        inv_copy(d).wait_recv()
        bin_quarter(d, bin_out)
        bin_copy(d).start()
        if d == 2:
            relay(1, 2)
        if d == 3:
            relay(1, 3)
    for t in range(4):
        relay(2, t)
    for t in range(4):
        relay(3, t)

    block = 16 * length
    r = lax.broadcasted_iota(jnp.int32, (block, block), 0)
    c = lax.broadcasted_iota(jnp.int32, (block, block), 1)
    turn = jnp.logical_and(
        lax.div(r, length) == lax.rem(c, 16), lax.rem(r, length) == lax.div(c, 16)
    ).astype(jnp.bfloat16)
    for d in range(1, 4):
        bin_copy(d).wait_recv()
    for n in range(quarter // 16):
        pieces = []
        for owner in range(seq_count):
            slot = owner + seq - 2 * (
                lax.rem(owner, 2) * lax.rem(seq, 2) + 2 * (owner // 2) * lax.div(seq, 2)
            )
            for b in range(bins):
                pieces.append(bin_in[slot, b * quarter + n * 16 : b * quarter + n * 16 + 16, :])
        turned = jnp.dot(
            turn, jnp.concatenate(pieces, axis=0), preferred_element_type=jnp.float32
        ).astype(jnp.bfloat16)
        at = slice(n * block, (n + 1) * block)
        spread[at, :] = mask[at, :] * jnp.concatenate([turned] * sessions, axis=1)

    def project(owner):
        at = pl.ds(pl.multiple_of(owner * columns, 128), columns)
        weights = folded[owner].reshape(sessions * CH, columns)
        qkv_ref[:, at] = jnp.dot(
            spread[...], weights, preferred_element_type=jnp.float32
        ).astype(jnp.bfloat16)

    project(seq)
    project(seq + flip_x)
    for line in range(4):
        for t in range(4):
            at = piece(line, t)
            fold_copy((at[0] + 1 - 2 * core, at[1]), 0, other_core).wait_recv()
    project(seq + 1 - 2 * core)
    project(seq + flip_x + 1 - 2 * core)

    for d in range(1, 4):
        square_copy(d).wait_send()
        inv_copy(d).wait_send()
        bin_copy(d).wait_send()
    for line in range(4):
        for t in range(4):
            if line == 0:
                along_z(t, wait_send)
            onward(line, t, wait_send)


def attention(qkv_ref, out_ref):
    patches, length, _ = out_ref.shape
    block = patches * length
    group = HEADS // KVH
    same = lax.div(lax.broadcasted_iota(jnp.int32, (group * block, block), 0), length)
    same = lax.rem(same, patches) == lax.div(
        lax.broadcasted_iota(jnp.int32, (group * block, block), 1), length
    )

    def normed(h, scale):
        values = qkv_ref[:, h * HD : (h + 1) * HD].astype(jnp.float32)
        mean = jnp.mean(values * values, axis=-1, keepdims=True)
        return (values * (lax.rsqrt(mean + 1e-06) * scale)).astype(jnp.bfloat16)

    for g in range(KVH):
        keys = normed(HEADS + g, 1.0)
        heads = range(g * group, (g + 1) * group)
        queries = jnp.concatenate([normed(h, HD**-0.5) for h in heads], axis=0)
        scores = lax.dot_general(
            queries, keys, (((1,), (1,)), ((), ())), preferred_element_type=jnp.float32
        )
        exponent = jnp.where(same, jnp.exp(scores), 0.0)
        weights = exponent * (1.0 / jnp.sum(exponent, axis=-1, keepdims=True))
        mixed = jnp.dot(
            weights.astype(jnp.bfloat16),
            qkv_ref[:, (HEADS + KVH + g) * HD : (HEADS + KVH + g + 1) * HD],
            preferred_element_type=jnp.float32,
        )
        for i, h in enumerate(heads):
            own_rows = mixed[i * block : (i + 1) * block].reshape(patches, length, HD)
            out_ref[:, :, h * HD : (h + 1) * HD] = own_rows.astype(
                jnp.bfloat16
            )


def fused(power, bin_index, session, readin_weight, qkv_weight):
    samples, channels = power.shape
    seq_count, sessions = lax.axis_size("seq"), lax.axis_size("wide")
    quarter = channels // CH // seq_count
    bins = samples // SPB
    columns = qkv_weight.shape[1] // seq_count
    rows = quarter * bins * seq_count
    width = readin_weight.shape[2]
    hbm = pl.BlockSpec(memory_space=pltpu.HBM)
    vmem = pl.BlockSpec(memory_space=pltpu.VMEM)
    bf16, f32 = jnp.bfloat16, jnp.float32
    dma = pltpu.SemaphoreType.DMA
    qkv = pl.pallas_call(
        kernel,
        out_shape=jax.ShapeDtypeStruct((rows, qkv_weight.shape[1]), bf16),
        in_specs=[hbm] * 5,
        out_specs=vmem,
        scratch_shapes=[
            pltpu.VMEM((1, samples), jnp.int32),
            pltpu.VMEM((session.shape[0] // 128, 128), jnp.int32),
            pltpu.VMEM((samples, channels), bf16),
            pltpu.VMEM((CH, width), bf16),
            pltpu.VMEM((width, columns), bf16),
            pltpu.VMEM((seq_count, sessions, CH, columns), bf16),
            pltpu.VMEM((rows, sessions * CH), bf16),
            pltpu.VMEM((rows, sessions * CH), bf16),
            pltpu.VMEM((seq_count, quarter, CH), f32),
            pltpu.VMEM((seq_count, quarter, CH), f32),
            pltpu.VMEM((seq_count, quarter, CH), f32),
            pltpu.VMEM((seq_count, bins * quarter, CH), bf16),
            pltpu.VMEM((seq_count, bins * quarter, CH), bf16),
            dma((8,)),
            dma((36,)),
            dma((seq_count, sessions)),
            dma((3, seq_count)),
            dma((3, seq_count)),
        ],
        compiler_params=pltpu.CompilerParams(
            collective_id=0, has_side_effects=True, vmem_limit_bytes=56 * 2**20
        ),
    )(power, bin_index.reshape(1, samples), session.reshape(-1, 128), readin_weight, qkv_weight)
    length = bins * seq_count
    return pl.pallas_call(
        attention,
        grid=(quarter // 16,),
        out_shape=jax.ShapeDtypeStruct((quarter, length, HEADS * HD), bf16),
        in_specs=[pl.BlockSpec((16 * length, qkv.shape[1]), lambda n: (n, 0))],
        out_specs=pl.BlockSpec((16, length, HEADS * HD), lambda n: (n, 0, 0)),
    )(qkv)


def solution(mesh):
    fits = dict(mesh.shape) == {"wide": 8, "seq": 4}
    placed = (P("seq", "wide"), P("seq"), P(), P("wide", None, None), P())
    return jax.shard_map(
        fused if fits else body, mesh=mesh, in_specs=placed, out_specs=P(("wide", "seq"), None, None), check_vma=False
    )
```

```python
import jax
import jax.numpy as jnp
from jax import lax
from jax.experimental import pallas as pl
from jax.experimental.pallas import tpu as pltpu
from jax.sharding import PartitionSpec as P

CH = 128
HD = 128
HEADS = 8
KVH = 2
SPB = 20


def attention_rows(qkv, length):
    rows = qkv.shape[0]
    block = 16 * length
    group = HEADS // KVH
    values = qkv.astype(jnp.float32).reshape(rows, HEADS + 2 * KVH, HD)
    scored = values[:, : HEADS + KVH]
    normed = scored / jnp.sqrt(jnp.mean(scored * scored, axis=-1, keepdims=True) + 1e-06)
    normed = normed.astype(jnp.bfloat16).reshape(rows // block, block, HEADS + KVH, HD)
    queries = normed[:, :, :HEADS].reshape(rows // block, block, KVH, group, HD)
    scores = jnp.einsum(
        "nigrd,njgd->ngrij", queries, normed[:, :, HEADS:], preferred_element_type=jnp.float32
    ) / HD**0.5
    at = jnp.arange(block, dtype=jnp.int32) // length
    exponent = jnp.where(at[:, None] == at[None, :], jnp.exp(scores), 0.0)
    weights = (exponent / jnp.sum(exponent, axis=-1, keepdims=True)).astype(jnp.bfloat16)
    value_rows = qkv[:, (HEADS + KVH) * HD :].reshape(rows // block, block, KVH, HD)
    mixed = jnp.einsum(
        "ngrij,njgd->nigrd", weights, value_rows, preferred_element_type=jnp.float32
    )
    return mixed.astype(jnp.bfloat16).reshape(rows // length, length, HEADS * HD)


def body(power, bin_index, session, readin_weight, qkv_weight):
    wide_count = lax.axis_size("wide")
    seq_count = lax.axis_size("seq")
    wide_index = lax.axis_index("wide")
    seq_index = lax.axis_index("seq")
    sample_rows, channels = power.shape
    patch_count = channels // CH
    quarter = patch_count // seq_count
    bin_count = sample_rows // SPB
    columns = qkv_weight.shape[1] // seq_count

    signal = power.astype(jnp.float32)
    squares = lax.psum(jnp.sum(signal * signal, axis=0), "seq")
    inv_rms = 1.0 / jnp.sqrt(squares / (sample_rows * seq_count) + 1e-06)
    active = jnp.maximum(signal * inv_rms[None, :] - 0.8, 0.0)
    local_bins = bin_index - seq_index * bin_count
    onehot = (local_bins[:, None] == jnp.arange(bin_count, dtype=jnp.int32)[None, :]).astype(
        jnp.float32
    )
    binned = (jnp.dot(onehot.T, active, precision=lax.Precision.HIGHEST) * (1.0 / SPB)).astype(
        jnp.bfloat16
    )
    binned = binned.reshape(bin_count, seq_count, quarter, CH).transpose(1, 2, 0, 3)
    patches = lax.all_to_all(binned, "seq", split_axis=0, concat_axis=0, tiled=True)
    length = seq_count * bin_count
    rows = patches.transpose(1, 0, 2, 3).reshape(quarter, length, CH)
    owners = lax.dynamic_slice_in_dim(
        session, (wide_index * seq_count + seq_index) * quarter, quarter
    )
    marks = owners[:, None] == jnp.arange(wide_count, dtype=jnp.int32)[None, :]
    spread = jnp.where(marks[:, None, :, None], rows[:, :, None, :], jnp.bfloat16(0))
    spread = spread.reshape(quarter * length, wide_count * CH)

    def project(block):
        folded = jnp.dot(readin_weight[0], block, preferred_element_type=jnp.float32)
        folded = lax.all_gather(folded.astype(jnp.bfloat16), "wide", axis=0, tiled=True)
        return jnp.dot(spread, folded, preferred_element_type=jnp.float32).astype(jnp.bfloat16)

    if wide_count > 8:
        blocks = qkv_weight.reshape(qkv_weight.shape[0], seq_count, -1).transpose(1, 0, 2)
        qkv = lax.map(project, blocks).transpose(1, 0, 2).reshape(quarter * length, -1)
    else:
        qkv = project(qkv_weight)
    return attention_rows(qkv, length)


def kernel(
    power_hbm, bin_hbm, session_hbm, readin_hbm, weight_hbm, qkv_ref,
    bin_ref, session_ref,
    power_v, readin_v, weight_v, folded, mask, spread,
    sq_own, sq_in, inv, bin_out, bin_in,
    load_sem, fold_send, fold_recv, seq_send, seq_recv,
):
    wide, seq = lax.axis_index("wide"), lax.axis_index("seq")
    seq_count, quarter, _ = sq_own.shape
    samples, channels = power_v.shape
    sessions = folded.shape[1]
    columns = folded.shape[3]
    bins = bin_out.shape[1] // quarter
    length = bins * seq_count
    z, y = lax.div(wide, 2), lax.rem(wide, 2)
    x, core = lax.div(seq, 2), lax.rem(seq, 2)
    flip_y, flip_x = 1 - 2 * y, 2 - 4 * x

    def paired(index, t):
        return (index, index + 1 - 2 * lax.rem(index, 2), lax.rem(index + 2, 4), 3 - index)[t]

    loads = [
        pltpu.make_async_copy(readin_hbm.at[0], readin_v, load_sem.at[4]),
        pltpu.make_async_copy(
            weight_hbm.at[:, pl.ds(pl.multiple_of(seq * columns, 128), columns)],
            weight_v,
            load_sem.at[5],
        ),
    ]
    for load in loads:
        load.start()
    part = channels // seq_count

    def power_load(q):
        at = pl.ds(pl.multiple_of(q * part, 128), part)
        return pltpu.make_async_copy(power_hbm.at[:, at], power_v.at[:, at], load_sem.at[q])

    for q in range(seq_count):
        power_load(q).start()

    indices = [
        pltpu.make_async_copy(bin_hbm, bin_ref, load_sem.at[6]),
        pltpu.make_async_copy(session_hbm, session_ref, load_sem.at[7]),
    ]
    for load in indices:
        load.start()

    barrier = pltpu.get_barrier_semaphore()

    def greet(device):
        pl.semaphore_signal(
            barrier, inc=1, device_id=device, device_id_type=pl.DeviceIdType.MESH
        )

    for d in range(1, 4):
        greet((wide, paired(seq, d)))
    greet((wide + flip_y, seq))

    @pl.when(z > 0)
    def _():
        greet((wide - 2, seq))

    @pl.when(z < 3)
    def _():
        greet((wide + 2, seq))

    for load in loads:
        load.wait()
    folded[seq, wide] = jnp.dot(
        readin_v[...], weight_v[...], preferred_element_type=jnp.float32
    ).astype(jnp.bfloat16)

    peers = 4 + jnp.where(z > 0, 1, 0) + jnp.where(z < 3, 1, 0)
    pl.semaphore_wait(barrier, peers)

    first = (wide + (1 - core) * flip_y, seq + core * flip_x)
    second = (wide + core * flip_y, seq + (1 - core) * flip_x)
    other_core = (wide, seq + 1 - 2 * core)
    lines = (
        (seq, y),
        (first[1], lax.rem(first[0], 2)),
        (second[1], lax.rem(second[0], 2)),
        (seq + flip_x, 1 - y),
    )

    nearest = (z, 1 + lax.rem(z, 2), lax.rem(2 + 3 * z, 5), 3 - 3 * lax.div(z, 2))

    def piece(line, t):
        return lines[line][0], nearest[t] * 2 + lines[line][1]

    def fold_copy(at, sem, device):
        return pltpu.make_async_remote_copy(
            src_ref=folded.at[at[0], at[1]],
            dst_ref=folded.at[at[0], at[1]],
            send_sem=fold_send.at[sem],
            recv_sem=fold_recv.at[at[0], at[1]],
            device_id=device,
            device_id_type=pl.DeviceIdType.MESH,
        )

    def along_z(t, act):
        at = piece(0, t)
        here = nearest[t]

        @pl.when(jnp.logical_and(here <= z, z < 3))
        def _():
            act(fold_copy(at, t, (wide + 2, seq)))

        @pl.when(jnp.logical_and(here >= z, z > 0))
        def _():
            act(fold_copy(at, 4 + t, (wide - 2, seq)))

    def onward(line, t, act):
        at = piece(line, t)
        if line == 0:
            act(fold_copy(at, 8 + t, first))
        if line < 2:
            act(fold_copy(at, 12 + 4 * line + t, second))
        act(fold_copy(at, 20 + 4 * line + t, other_core))

    def start(copy):
        copy.start()

    def wait_send(copy):
        copy.wait_send()

    def relay(line, t):
        if line or t:
            fold_copy(piece(line, t), 0, other_core).wait_recv()
        if line == 0:
            along_z(t, start)
        onward(line, t, start)

    relay(0, 0)

    def seq_copy(kind, source, target, d):
        return pltpu.make_async_remote_copy(
            src_ref=source,
            dst_ref=target,
            send_sem=seq_send.at[kind, d],
            recv_sem=seq_recv.at[kind, d],
            device_id=(wide, paired(seq, d)),
            device_id_type=pl.DeviceIdType.MESH,
        )

    def patch_rows(q, c):
        at = pl.multiple_of(q * part + c * 16 * CH, 16 * CH)
        return power_v[:, pl.ds(at, 16 * CH)].astype(jnp.float32)

    def square_copy(d):
        return seq_copy(0, sq_own.at[paired(seq, d)], sq_in.at[d], d)

    for d in (2, 3, 1, 0):
        q = paired(seq, d)
        power_load(q).wait()

        @pl.loop(0, quarter // 16)
        def _(c):
            signal = patch_rows(q, c)
            signal = signal * signal
            sums = [
                jnp.sum(signal[:, k * CH : (k + 1) * CH], axis=0, keepdims=True) for k in range(16)
            ]
            sq_own[q, pl.ds(pl.multiple_of(c * 16, 16), 16), :] = jnp.concatenate(sums, axis=0)

        if d:
            square_copy(d).start()

    relay(0, 1)
    for load in indices:
        load.wait()

    rows = quarter * length
    device = wide * seq_count + seq
    session_row = session_ref[pl.ds(lax.div(device * quarter, 128), 1), :]
    named = (
        session_row == lax.broadcasted_iota(jnp.int32, (sessions, 128), 0)
    ).astype(jnp.bfloat16)
    lane = lax.broadcasted_iota(jnp.int32, (rows, 128), 1)
    row = lax.broadcasted_iota(jnp.int32, (rows, 128), 0)
    own = (
        lane == lax.rem(device * quarter, 128) + lax.div(row, length)
    ).astype(jnp.bfloat16)
    chosen = lax.dot_general(
        own, named, (((1,), (1,)), ((), ())), preferred_element_type=jnp.float32
    ).astype(jnp.bfloat16)
    widen = (
        lax.broadcasted_iota(jnp.int32, (sessions, sessions * CH), 0)
        == lax.div(lax.broadcasted_iota(jnp.int32, (sessions, sessions * CH), 1), CH)
    ).astype(jnp.bfloat16)
    mask[...] = jnp.dot(chosen, widen, preferred_element_type=jnp.float32).astype(jnp.bfloat16)

    diagonal = lax.broadcasted_iota(jnp.int32, (samples, samples), 0) == lax.broadcasted_iota(
        jnp.int32, (samples, samples), 1
    )
    local_bin = jnp.sum(
        jnp.where(diagonal, (bin_ref[...] - seq * bins).astype(jnp.float32), 0.0),
        axis=1,
        keepdims=True,
    )
    in_bin = [
        jnp.broadcast_to((local_bin == b).astype(jnp.float32), (samples, CH)) for b in range(bins)
    ]

    relay(0, 2)

    total = sq_own[seq]
    for d in range(1, 4):
        square_copy(d).wait_recv()
        total = total + sq_in[d]
    inv[0] = 1.0 / jnp.sqrt(total / (samples * seq_count) + 1e-06)

    def inv_copy(d):
        return seq_copy(1, inv.at[0], inv.at[d], d)

    for d in (2, 3, 1):
        inv_copy(d).start()

    def bin_quarter(d, target):
        q = paired(seq, d)

        @pl.loop(0, quarter // 16)
        def _(c):
            signal = patch_rows(q, c)
            at = pl.multiple_of(c * 16, 16)
            scale = inv[d, pl.ds(at, 16), :]
            found = [[] for _ in range(bins)]
            for k in range(16):
                active = jnp.maximum(
                    signal[:, k * CH : (k + 1) * CH] * scale[k : k + 1] - 0.8, 0.0
                )
                for b in range(bins):
                    found[b].append(jnp.sum(active * in_bin[b], axis=0, keepdims=True))
            for b in range(bins):
                target[d, pl.ds(pl.multiple_of(b * quarter + c * 16, 16), 16), :] = (
                    jnp.concatenate(found[b], axis=0) * (1.0 / SPB)
                ).astype(jnp.bfloat16)

    def bin_copy(d):
        return seq_copy(2, bin_out.at[d], bin_in.at[d], d)

    relay(0, 3)
    relay(1, 0)
    bin_quarter(0, bin_in)
    relay(1, 1)
    for d in (2, 3, 1):
        inv_copy(d).wait_recv()
        bin_quarter(d, bin_out)
        bin_copy(d).start()
        if d == 2:
            relay(1, 2)
        if d == 3:
            relay(1, 3)
    for t in range(4):
        relay(2, t)
    for t in range(4):
        relay(3, t)

    block = 16 * length
    r = lax.broadcasted_iota(jnp.int32, (block, block), 0)
    c = lax.broadcasted_iota(jnp.int32, (block, block), 1)
    turn = jnp.logical_and(
        lax.div(r, length) == lax.rem(c, 16), lax.rem(r, length) == lax.div(c, 16)
    ).astype(jnp.bfloat16)
    for d in range(1, 4):
        bin_copy(d).wait_recv()
    for n in range(quarter // 16):
        pieces = []
        for owner in range(seq_count):
            slot = owner + seq - 2 * (
                lax.rem(owner, 2) * lax.rem(seq, 2) + 2 * (owner // 2) * lax.div(seq, 2)
            )
            for b in range(bins):
                pieces.append(bin_in[slot, b * quarter + n * 16 : b * quarter + n * 16 + 16, :])
        turned = jnp.dot(
            turn, jnp.concatenate(pieces, axis=0), preferred_element_type=jnp.float32
        ).astype(jnp.bfloat16)
        at = slice(n * block, (n + 1) * block)
        spread[at, :] = mask[at, :] * jnp.concatenate([turned] * sessions, axis=1)

    def project(owner):
        at = pl.ds(pl.multiple_of(owner * columns, 128), columns)
        weights = folded[owner].reshape(sessions * CH, columns)
        qkv_ref[:, at] = jnp.dot(
            spread[...], weights, preferred_element_type=jnp.float32
        ).astype(jnp.bfloat16)

    project(seq)
    project(seq + flip_x)
    for line in range(4):
        for t in range(4):
            at = piece(line, t)
            fold_copy((at[0] + 1 - 2 * core, at[1]), 0, other_core).wait_recv()
    project(seq + 1 - 2 * core)
    project(seq + flip_x + 1 - 2 * core)

    for d in range(1, 4):
        square_copy(d).wait_send()
        inv_copy(d).wait_send()
        bin_copy(d).wait_send()
    for line in range(4):
        for t in range(4):
            if line == 0:
                along_z(t, wait_send)
            onward(line, t, wait_send)


def attention(qkv_ref, out_ref):
    patches, length, _ = out_ref.shape
    block = patches * length
    group = HEADS // KVH
    same = lax.div(lax.broadcasted_iota(jnp.int32, (group * block, block), 0), length)
    same = lax.rem(same, patches) == lax.div(
        lax.broadcasted_iota(jnp.int32, (group * block, block), 1), length
    )

    ones = jnp.ones((HD, HD), jnp.bfloat16)

    def normed(h, scale):
        values = qkv_ref[:, h * HD : (h + 1) * HD].astype(jnp.float32)
        total = jnp.dot(
            (values * values).astype(jnp.bfloat16), ones, preferred_element_type=jnp.float32
        )
        return (values * (lax.rsqrt(total / HD + 1e-06) * scale)).astype(jnp.bfloat16)

    for g in range(KVH):
        keys = normed(HEADS + g, 1.0)
        heads = range(g * group, (g + 1) * group)
        queries = jnp.concatenate([normed(h, HD**-0.5) for h in heads], axis=0)
        scores = lax.dot_general(
            queries, keys, (((1,), (1,)), ((), ())), preferred_element_type=jnp.float32
        )
        exponent = jnp.where(same, jnp.exp(scores), 0.0)
        values = qkv_ref[:, (HEADS + KVH + g) * HD : (HEADS + KVH + g + 1) * HD]
        summed = jnp.dot(
            exponent.astype(jnp.bfloat16),
            jnp.concatenate([values, ones[:block]], axis=1),
            preferred_element_type=jnp.float32,
        )
        mixed = summed[:, :HD] * (1.0 / summed[:, HD:])
        for i, h in enumerate(heads):
            own_rows = mixed[i * block : (i + 1) * block].reshape(patches, length, HD)
            out_ref[:, :, h * HD : (h + 1) * HD] = own_rows.astype(
                jnp.bfloat16
            )


def fused(power, bin_index, session, readin_weight, qkv_weight):
    samples, channels = power.shape
    seq_count, sessions = lax.axis_size("seq"), lax.axis_size("wide")
    quarter = channels // CH // seq_count
    bins = samples // SPB
    columns = qkv_weight.shape[1] // seq_count
    rows = quarter * bins * seq_count
    width = readin_weight.shape[2]
    hbm = pl.BlockSpec(memory_space=pltpu.HBM)
    vmem = pl.BlockSpec(memory_space=pltpu.VMEM)
    bf16, f32 = jnp.bfloat16, jnp.float32
    dma = pltpu.SemaphoreType.DMA
    qkv = pl.pallas_call(
        kernel,
        out_shape=jax.ShapeDtypeStruct((rows, qkv_weight.shape[1]), bf16),
        in_specs=[hbm] * 5,
        out_specs=vmem,
        scratch_shapes=[
            pltpu.VMEM((1, samples), jnp.int32),
            pltpu.VMEM((session.shape[0] // 128, 128), jnp.int32),
            pltpu.VMEM((samples, channels), bf16),
            pltpu.VMEM((CH, width), bf16),
            pltpu.VMEM((width, columns), bf16),
            pltpu.VMEM((seq_count, sessions, CH, columns), bf16),
            pltpu.VMEM((rows, sessions * CH), bf16),
            pltpu.VMEM((rows, sessions * CH), bf16),
            pltpu.VMEM((seq_count, quarter, CH), f32),
            pltpu.VMEM((seq_count, quarter, CH), f32),
            pltpu.VMEM((seq_count, quarter, CH), f32),
            pltpu.VMEM((seq_count, bins * quarter, CH), bf16),
            pltpu.VMEM((seq_count, bins * quarter, CH), bf16),
            dma((8,)),
            dma((36,)),
            dma((seq_count, sessions)),
            dma((3, seq_count)),
            dma((3, seq_count)),
        ],
        compiler_params=pltpu.CompilerParams(
            collective_id=0, has_side_effects=True, vmem_limit_bytes=56 * 2**20
        ),
    )(power, bin_index.reshape(1, samples), session.reshape(-1, 128), readin_weight, qkv_weight)
    length = bins * seq_count
    return pl.pallas_call(
        attention,
        grid=(quarter // 16,),
        out_shape=jax.ShapeDtypeStruct((quarter, length, HEADS * HD), bf16),
        in_specs=[pl.BlockSpec((16 * length, qkv.shape[1]), lambda n: (n, 0))],
        out_specs=pl.BlockSpec((16, length, HEADS * HD), lambda n: (n, 0, 0)),
    )(qkv)


def solution(mesh):
    fits = dict(mesh.shape) == {"wide": 8, "seq": 4}
    placed = (P("seq", "wide"), P("seq"), P(), P("wide", None, None), P())
    return jax.shard_map(
        fused if fits else body, mesh=mesh, in_specs=placed, out_specs=P(("wide", "seq"), None, None), check_vma=False
    )
```
